32 devices in a mesh: gx: 8 (over z, y), gy: 4 (over x, core).
Axes of the slice: x: 2, y: 2, z: 4, core: 2. Of those that a mesh axis runs over, the one named last changes fastest.
Arguments:
- density: bfloat16 [8, 4, 3, 20, 128, 128], P('gx', 'gy'), may hold values from -0.3 to 0.8
- neighbours: int32 [8, 4, 3, 20], replicated, may hold values from 0 to 95, as said below
- ent_blocks: bfloat16 [768, 128, 128], P(('gx', 'gy')), may hold values from -0.59765625 to 0.59765625
- ent_owner: int32 [768], replicated, may hold values from 0 to 31, as said below
- ent_place: int32 [768], replicated, may hold values from 0 to 59
Outputs:
- purified: float32 [8, 4, 3, 20, 128, 128], P('gx', 'gy')
The draws below stay inside these ranges and needn't reach their ends.
Inputs may be any that keep to these rules, and one draw needn't show every extreme that they name: neighbours[x, y, r, 0] is the row's own index (x * 4 + y) * 3 + r; the other 19 entries of a row are distinct rows of devices (x + a mod 8, y + b mod 4) with a and b in -1, 0, 1. `ent_owner`: among the 24 entries d * 24 to d * 24 + 23 of one device d, no owner is named more than 2 times, and some owner exactly 2 times.
All inputs are finite; a program needn't handle non-finite values.
Results may differ from the reference program's by a relative error of at most 0.0059.
Values may be sent and summed in bfloat16 or wider, within the bound.
A program may use at most 128 MiB of HBM per device.

```python
import jax
import jax.numpy as jnp
from jax import lax

B = 128
K = 20
R = 3
C = 2
SLAB_X = 8
SLAB_Y = 4
NDEV = 32
E = 24


def draw_density(key, part):
    shape_all = (SLAB_X, SLAB_Y, R, K, B, B)
    orbital_ids = jnp.arange(B, dtype=jnp.int32)
    unit_diag = (orbital_ids[:, None] == orbital_ids[None, :]).astype(jnp.float32)
    slot_ids = jnp.arange(K, dtype=jnp.int32)
    own_slot = (slot_ids == 0).astype(jnp.float32)
    base_part = 0.5 * own_slot[None, None, None, :, None, None] * unit_diag[None, None, None, None, :, :]
    noise_part = 0.05 * jnp.clip(jax.random.normal(key, shape_all, jnp.float32), -6.0, 6.0)
    return (base_part + noise_part).astype(jnp.bfloat16)


def draw_neighbours(key, part):
    total_rows = NDEV * R
    candidates = 9 * R
    global_ids = jnp.arange(total_rows, dtype=jnp.int32)
    home_x = global_ids // (SLAB_Y * R)
    home_y = global_ids // R % SLAB_Y
    home_r = global_ids % R
    row_keys = jax.random.split(key, total_rows)

    def shuffled(row_key):
        return jax.random.permutation(row_key, candidates - 1)
    choices_made = jax.vmap(shuffled)(row_keys)[:, :K - 1].astype(jnp.int32)
    self_slot = 4 * R + home_r
    picked = jnp.where(choices_made >= self_slot[:, None], choices_made + 1, choices_made)
    near_device = picked // R
    near_row = picked % R
    delta_x = near_device // 3 - 1
    delta_y = near_device % 3 - 1
    column_x = (home_x[:, None] + delta_x) % SLAB_X
    column_y = (home_y[:, None] + delta_y) % SLAB_Y
    columns = (column_x * SLAB_Y + column_y) * R + near_row
    joined = jnp.concatenate([global_ids[:, None], columns], axis=1)
    return joined.reshape(SLAB_X, SLAB_Y, R, K).astype(jnp.int32)


def draw_ent_owner(key, part):
    hot_owner = jax.random.randint(jax.random.fold_in(key, 7), (), 0, NDEV)
    source_keys = jax.random.split(jax.random.fold_in(key, 11), NDEV)

    def one_source(source_key):
        first_key, second_key = jax.random.split(source_key)
        others = jax.random.permutation(first_key, (NDEV - 1) * C)[:E - C] + C
        values = jnp.concatenate([jnp.arange(C, dtype=jnp.int32), others.astype(jnp.int32)])
        order = jax.random.permutation(second_key, E)
        values = values[order]
        return (values // C + hot_owner) % NDEV
    return jax.vmap(one_source)(source_keys).reshape(-1).astype(jnp.int32)


def place_ends(entries, own_key, smallest, high):
    extent = entries.shape
    spot = [jax.random.randint(jax.random.fold_in(own_key, axis), (), 0, extent[axis]) for axis in range(len(extent))]
    entries = entries.at[tuple(spot)].set(smallest)
    longest = extent.index(max(extent))
    spot[longest] = (spot[longest] + 1) % extent[longest]
    return entries.at[tuple(spot)].set(high)


def levels(stream_key, dims, cuts, low, high):
    gain, own = 1.0, jax.random.fold_in(stream_key, 6)
    for dim, shards_of in cuts:
        draws = jnp.exp(jax.random.uniform(jax.random.fold_in(own, dim), (shards_of,), jnp.float32, low / len(cuts), high / len(cuts)))
        gain = gain * jnp.repeat(draws, dims[dim] // shards_of).reshape([-1 if axis == dim else 1 for axis in range(len(dims))])
    return gain


def centred(own_key, shape, deviation, most, pieces=(), held_as=jnp.bfloat16):
    values = deviation * jax.random.normal(own_key, shape, jnp.float32)
    if pieces:
        values = values * levels(own_key, shape, pieces, -0.22, 0.18)
    return jnp.clip(values, -most, most).astype(held_as)


def setup_inputs(seed: int = 0) -> dict:
    splits = jax.random.split(jax.random.key(seed), 6)
    density = draw_density(jax.random.fold_in(splits[5], 71), 0)
    neighbours = draw_neighbours(jax.random.fold_in(splits[5], 71), 0)
    ent_blocks = centred(splits[2], (NDEV * E, B, B), 0.1, 0.59765625, ((0, 32),))
    ent_owner = draw_ent_owner(jax.random.fold_in(splits[5], 71), 0)
    ent_place = place_ends(jax.random.randint(splits[4], (NDEV * E,), 0, R * K), jax.random.fold_in(splits[4], 1), 0, (R * K) - 1).astype(jnp.int32)
    return dict(density=density, neighbours=neighbours, ent_blocks=ent_blocks, ent_owner=ent_owner, ent_place=ent_place)


def block_positions(neighbours, here_x, here_y, row_columns):
    wide_count, narrow_count, row_count, slot_count = neighbours.shape
    listing = neighbours.reshape(wide_count * narrow_count * row_count, slot_count)
    inner_lists = jnp.take(listing, row_columns, axis=0)
    matches = inner_lists[:, None, :] == row_columns[None, :, None]
    present = jnp.any(matches, axis=2)
    slot_ids = jnp.arange(slot_count, dtype=jnp.int32)
    inner_slot = jnp.sum(jnp.where(matches, slot_ids[None, None, :], 0), axis=2).astype(jnp.int32)
    inner_x = row_columns // (narrow_count * row_count)
    inner_y = (row_columns // row_count) % narrow_count
    inner_r = row_columns % row_count
    near_x = (inner_x - here_x + 1) % wide_count
    near_y = (inner_y - here_y + 1) % narrow_count
    near_row = (near_x * 3 + near_y) * row_count + inner_r
    position = near_row[:, None] * slot_count + inner_slot
    return jnp.where(present, position, 9 * row_count * slot_count).astype(jnp.int32)


def reference(density, neighbours, ent_blocks, ent_owner, ent_place):
    area = B * B
    flat_blocks = density.reshape(NDEV * R * K, area).astype(jnp.float32)
    owners = ent_owner.reshape(NDEV, E)
    places = ent_place.reshape(NDEV, E)
    entering = ent_blocks.reshape(NDEV, E, area)

    def add_source(total, item):
        owner_list, place_list, block_list = item
        target = (owner_list * (R * K) + place_list).astype(jnp.int32)
        return total.at[target].add(block_list.astype(jnp.float32)), None

    flat_blocks, unused = lax.scan(add_source, flat_blocks, (owners, places, entering))
    admitted = flat_blocks.astype(jnp.bfloat16).reshape(SLAB_X, SLAB_Y, R, K, B, B)
    admitted = lax.optimization_barrier(admitted)

    def one_device(device_id):
        here_x = device_id // SLAB_Y
        here_y = device_id % SLAB_Y
        offsets = jnp.arange(3, dtype=jnp.int32) - 1
        near_xs = ((here_x + offsets) % SLAB_X).astype(jnp.int32)
        near_ys = ((here_y + offsets) % SLAB_Y).astype(jnp.int32)
        table = jnp.take(jnp.take(admitted, near_xs, axis=0), near_ys, axis=1)
        table = table.reshape(9 * R * K, B, B).astype(jnp.float32)
        own_rows = admitted[here_x, here_y]
        own_columns = neighbours[here_x, here_y]

        def one_row(item):
            left_blocks, row_columns = item
            position = block_positions(neighbours, here_x, here_y, row_columns)
            gathered = jnp.take(table, position.reshape(-1), axis=0, mode="fill", fill_value=0.0)
            gathered = gathered.reshape(K, K, B, B)
            square = jnp.einsum("mab,mkbc->kac", left_blocks.astype(jnp.float32), gathered)
            square_b = lax.optimization_barrier(square.astype(jnp.bfloat16))
            cube = jnp.einsum("mab,mkbc->kac", square_b.astype(jnp.float32), gathered)
            return 3.0 * square - 2.0 * cube

        return lax.map(one_row, (own_rows, own_columns))

    result = lax.map(one_device, jnp.arange(NDEV, dtype=jnp.int32))
    return result.reshape(SLAB_X, SLAB_Y, R, K, B, B)
```

```python
import functools

import jax
import jax.numpy as jnp
from jax import lax
from jax.experimental import pallas as pl
from jax.experimental.pallas import tpu as pltpu
from jax.sharding import PartitionSpec as P

C = 2
MIB = 1024 * 1024


def pack_kernel(index_ref, ent_ref, out_ref):
    def body(i, carry):
        out_ref[i] = ent_ref[index_ref[i]]
        return carry

    lax.fori_loop(0, out_ref.shape[0], body, 0)


def admit_kernel(place_ref, inverse_ref, received_ref, density_ref, own_ref, total):
    rows, slots = inverse_ref.shape[0], density_ref.shape[0] // inverse_ref.shape[0]
    width = density_ref.shape[1]

    def widen(i, carry):
        total[i] = density_ref[i].astype(jnp.float32)
        return carry

    lax.fori_loop(0, density_ref.shape[0], widen, 0)

    def add(j, carry):
        place = place_ref[j]

        @pl.when(place >= 0)
        def _():
            total[place] += received_ref[j].astype(jnp.float32)

        return carry

    lax.fori_loop(0, received_ref.shape[0], add, 0)

    def spread(near, carry):
        for r in range(rows):
            for c in range(rows):
                slot = inverse_ref[r, near * rows + c]
                spot = (near, pl.ds(r * width, width), pl.ds(c * width, width))

                @pl.when(slot >= 0)
                def _():
                    own_ref[spot] = total[r * slots + slot].astype(jnp.bfloat16)

                @pl.when(slot < 0)
                def _():
                    own_ref[spot] = jnp.zeros((width, width), jnp.bfloat16)

        return carry

    lax.fori_loop(0, 9, spread, 0)


def purify_kernel(pieces_of, rows, slots, inverse_ref, *refs):
    count = 1 + max(p for p, _ in pieces_of.values())
    pieces = refs[:count]
    out_ref, left, right, square, square_b, sem = refs[count:]
    side = left.shape[0]
    width = side // rows
    copies = []
    for near in range(9):
        copies.append(
            pltpu.make_async_copy(
                pieces[0].at[near], left.at[:, pl.ds(near * side, side)], sem.at[len(copies)]
            )
        )
    for (m, c), (p, spot) in pieces_of.items():
        copies.append(
            pltpu.make_async_copy(
                pieces[p].at[spot], right.at[c, pl.ds(m * side, side), :], sem.at[len(copies)]
            )
        )
    for copy in copies:
        copy.start()
    for copy in copies:
        copy.wait()

    def product(lhs, c):
        cx, cy = c // 3, c % 3
        low_x, high_x = max(cx - 1, 0), min(cx + 1, 2)
        if cy == 1:
            spans = [(low_x * 3, (high_x + 1) * 3)]
        else:
            low_y, high_y = max(cy - 1, 0), min(cy + 1, 2)
            spans = [(mx * 3 + low_y, mx * 3 + high_y + 1) for mx in range(low_x, high_x + 1)]
        total = None
        for start, stop in spans:
            span = pl.ds(start * side, (stop - start) * side)
            term = jnp.dot(
                lhs[:, span], right[c, span, :], preferred_element_type=jnp.float32
            )
            total = term if total is None else total + term
        return total

    for c in range(9):
        square[c] = product(left, c)
        for r in range(rows):
            for q in range(rows):
                listed = inverse_ref[r, c * rows + q] >= 0
                down, across = pl.ds(r * width, width), pl.ds(q * width, width)
                tile = square[c, down, across]
                square_b[down, pl.ds(c * side + q * width, width)] = jnp.where(
                    listed, tile, jnp.zeros_like(tile)
                ).astype(jnp.bfloat16)
    for c in range(9):
        square[c] = 3.0 * square[c] - 2.0 * product(square_b, c)
        for r in range(rows):
            for q in range(rows):
                slot = inverse_ref[r, c * rows + q]

                @pl.when(slot >= 0)
                def _():
                    out_ref[r * slots + slot] = square[
                        c, pl.ds(r * width, width), pl.ds(q * width, width)
                    ]


def in_vmem():
    return pl.BlockSpec(memory_space=pltpu.VMEM)


def in_smem():
    return pl.BlockSpec(memory_space=pltpu.SMEM)


def shift(cells, axis, step):
    count = lax.axis_size(axis)
    return lax.ppermute(cells, axis, [(i, (i + step) % count) for i in range(count)])


def per_device(density, neighbours, ent_blocks, ent_owner, ent_place):
    wide_count = lax.axis_size("gx")
    narrow_count = lax.axis_size("gy")
    device_count = wide_count * narrow_count
    here_x = lax.axis_index("gx")
    here_y = lax.axis_index("gy")
    self_index = here_x * narrow_count + here_y
    rows, slots, width = density.shape[2:5]
    side = rows * width
    held = ent_blocks.shape[0]

    owners = ent_owner.reshape(device_count, held)
    places = ent_place.reshape(device_count, held)
    entry_ids = jnp.arange(held, dtype=jnp.int32)
    my_owners = lax.dynamic_index_in_dim(owners, self_index, 0, False)
    earlier = entry_ids[None, :] < entry_ids[:, None]
    my_ranks = jnp.sum((my_owners[:, None] == my_owners[None, :]) & earlier, axis=1)
    send_slot = my_owners * C + my_ranks
    buffer_ids = jnp.arange(device_count * C, dtype=jnp.int32)
    send_index = jnp.sum(
        jnp.where(buffer_ids[:, None] == send_slot[None, :], entry_ids[None, :], 0), axis=1
    ).astype(jnp.int32)
    for_me = owners == self_index
    my_rank_at = jnp.sum(for_me[:, None, :] & earlier[None, :, :], axis=2)
    capacity_ids = jnp.arange(C, dtype=jnp.int32)
    picked = for_me[:, :, None] & (my_rank_at[:, :, None] == capacity_ids[None, None, :])
    slot_place = (
        jnp.sum(jnp.where(picked, places[:, :, None] + 1, 0), axis=1).reshape(-1) - 1
    ).astype(jnp.int32)

    columns = lax.dynamic_index_in_dim(
        lax.dynamic_index_in_dim(neighbours, here_x, 0, False), here_y, 0, False
    )
    near_x = (columns // (narrow_count * rows) - here_x + 1) % wide_count
    near_y = (columns // rows % narrow_count - here_y + 1) % narrow_count
    spot = (near_x * 3 + near_y) * rows + columns % rows
    slot_ids = jnp.arange(slots, dtype=jnp.int32)
    spot_ids = jnp.arange(9 * rows, dtype=jnp.int32)
    inverse = (
        jnp.sum(
            jnp.where(spot[:, :, None] == spot_ids[None, None, :], slot_ids[None, :, None] + 1, 0),
            axis=1,
        )
        - 1
    ).astype(jnp.int32)

    outgoing = pl.pallas_call(
        pack_kernel,
        out_shape=jax.ShapeDtypeStruct((device_count * C, width, width), jnp.bfloat16),
        in_specs=[in_smem(), in_vmem()],
        out_specs=in_vmem(),
        compiler_params=pltpu.CompilerParams(vmem_limit_bytes=32 * MIB),
        name="pack",
    )(send_index, ent_blocks)
    received = lax.all_to_all(outgoing, ("gx", "gy"), split_axis=0, concat_axis=0, tiled=True)
    own = pl.pallas_call(
        admit_kernel,
        out_shape=jax.ShapeDtypeStruct((9, side, side), jnp.bfloat16),
        in_specs=[in_smem(), in_smem(), in_vmem(), in_vmem()],
        out_specs=in_vmem(),
        scratch_shapes=[pltpu.VMEM((rows * slots, width, width), jnp.float32)],
        compiler_params=pltpu.CompilerParams(vmem_limit_bytes=40 * MIB),
        name="admit",
    )(slot_place, inverse, received, density.reshape(rows * slots, width, width))

    own_grid = own.reshape(3, 3, side, side)
    pieces, pieces_of = [own], {(4, c): (0, (c,)) for c in range(9)}

    def keep(piece, mx, my, column_xs, column_ys):
        pieces.append(piece)
        for i, cx in enumerate(column_xs):
            for j, cy in enumerate(column_ys):
                pieces_of[(mx * 3 + my, cx * 3 + cy)] = (len(pieces) - 1, (i, j))

    for step in (1, -1):
        low = 1 if step == 1 else 0
        sent = lax.slice_in_dim(own_grid, low, low + 2, axis=1)
        keep(shift(sent, "gy", step), 1, 1 - step, (0, 1, 2), (1 - low, 2 - low))
    for part in (0, 1):
        for step_x in (1, -1):
            low_x = 1 if step_x == 1 else 0
            sent = lax.slice_in_dim(own_grid, low_x + part, low_x + part + 1, axis=0)
            edge = shift(sent, "gx", step_x)
            cx = low_x + part + (-1 if step_x == 1 else 1)
            mx = 1 - step_x
            keep(edge, mx, 1, (cx,), (0, 1, 2))
            for step in (1, -1):
                low = 1 if step == 1 else 0
                corner = lax.slice_in_dim(edge, low, low + 2, axis=1)
                keep(shift(corner, "gy", step), mx, 1 - step, (cx,), (1 - low, 2 - low))
    return run_purify(pieces, pieces_of, inverse, rows, slots, width, density.shape)


def run_purify(pieces, pieces_of, inverse, rows, slots, width, shape):
    side = rows * width
    purified = pl.pallas_call(
        functools.partial(purify_kernel, pieces_of, rows, slots),
        out_shape=jax.ShapeDtypeStruct((rows * slots, width, width), jnp.float32),
        in_specs=[in_smem()] + [pl.BlockSpec(memory_space=pl.ANY)] * len(pieces),
        out_specs=in_vmem(),
        scratch_shapes=[
            pltpu.VMEM((side, 9 * side), jnp.bfloat16),
            pltpu.VMEM((9, 9 * side, side), jnp.bfloat16),
            pltpu.VMEM((9, side, side), jnp.float32),
            pltpu.VMEM((side, 9 * side), jnp.bfloat16),
            pltpu.SemaphoreType.DMA((9 + len(pieces_of),)),
        ],
        compiler_params=pltpu.CompilerParams(vmem_limit_bytes=56 * MIB),
        name="purify",
    )(inverse, *pieces)
    return purified.reshape(shape)


def solution(mesh):
    in_specs = (P("gx", "gy", None, None, None, None), P(), P(("gx", "gy"), None, None), P(), P())
    out_specs = P("gx", "gy", None, None, None, None)
    return jax.shard_map(
        per_device, mesh=mesh, in_specs=in_specs, out_specs=out_specs, check_vma=False
    )
```

```python
import functools

import jax
import jax.numpy as jnp
from jax import lax
from jax.experimental import pallas as pl
from jax.experimental.pallas import tpu as pltpu
from jax.sharding import PartitionSpec as P

C = 2
MIB = 1024 * 1024


def pack_kernel(index_ref, ent_ref, out_ref):
    def body(i, carry):
        out_ref[i] = ent_ref[index_ref[i]]
        return carry

    lax.fori_loop(0, out_ref.shape[0], body, 0)


def admit_kernel(place_ref, inverse_ref, received_ref, density_ref, own_ref, total):
    rows, slots = inverse_ref.shape[0], density_ref.shape[0] // inverse_ref.shape[0]
    width = density_ref.shape[1]

    def widen(i, carry):
        total[i] = density_ref[i].astype(jnp.float32)
        return carry

    lax.fori_loop(0, density_ref.shape[0], widen, 0)

    def add(j, carry):
        place = place_ref[j]

        @pl.when(place >= 0)
        def _():
            total[place] += received_ref[j].astype(jnp.float32)

        return carry

    lax.fori_loop(0, received_ref.shape[0], add, 0)

    def spread(near, carry):
        for r in range(rows):
            for c in range(rows):
                slot = inverse_ref[r, near * rows + c]
                spot = (near, pl.ds(r * width, width), pl.ds(c * width, width))

                @pl.when(slot >= 0)
                def _():
                    own_ref[spot] = total[r * slots + slot].astype(jnp.bfloat16)

                @pl.when(slot < 0)
                def _():
                    own_ref[spot] = jnp.zeros((width, width), jnp.bfloat16)

        return carry

    lax.fori_loop(0, 9, spread, 0)


def exchange_kernel(
    rows, gx_count, gy_count, own_ref, mask_ref, out_ref,
    left, right, square, square_b, local_sem, send_sem, recv_sem,
):
    side = left.shape[0]
    width = side // rows
    here_x, here_y = lax.axis_index("gx"), lax.axis_index("gy")
    beside_x = {
        1: (lax.rem(here_x + 1, gx_count), here_y),
        -1: (lax.rem(here_x + gx_count - 1, gx_count), here_y),
    }
    beside_y = {
        1: (here_x, lax.rem(here_y + 1, gy_count)),
        -1: (here_x, lax.rem(here_y + gy_count - 1, gy_count)),
    }

    def tile(c, m):
        return right.at[c, pl.ds(m * side, side), :]

    local = [
        pltpu.make_async_copy(own_ref.at[m], left.at[:, pl.ds(m * side, side)], local_sem.at[m])
        for m in range(9)
    ] + [
        pltpu.make_async_copy(own_ref.at[c], tile(c, 4), local_sem.at[9 + c]) for c in range(9)
    ]

    sends = []

    def send(source, c, m, device):
        copy = pltpu.make_async_remote_copy(
            src_ref=source,
            dst_ref=tile(c, m),
            send_sem=send_sem.at[len(sends)],
            recv_sem=recv_sem.at[len(sends)],
            device_id=device,
            device_id_type=pl.DeviceIdType.MESH,
        )
        sends.append(copy)
        copy.start()
        return copy

    barrier = pltpu.get_barrier_semaphore()
    for device in (*beside_x.values(), *beside_y.values()):
        pl.semaphore_signal(barrier, inc=1, device_id=device, device_id_type=pl.DeviceIdType.MESH)
    pl.semaphore_wait(barrier, 4)

    edges, sides = [], []
    for qy in (1, 0, 2):
        for part in (0, 1):
            for step in (1, -1):
                qx = part + 1 if step == 1 else part
                cx, mx = qx - step, 1 - step
                copy = send(own_ref.at[qx * 3 + qy], cx * 3 + qy, mx * 3 + 1, beside_x[step])
                edges.append((copy, cx, qy, mx))
                qy2 = part + 1 if step == 1 else part
                line = (1, 0, 2).index(qy)
                c2 = line * 3 + qy2 - step
                sides.append(send(own_ref.at[line * 3 + qy2], c2, 3 + 1 - step, beside_y[step]))
    for copy in local:
        copy.start()

    corners = []

    def forward(edge):
        copy, cx, cy, mx = edge
        copy.wait_recv()
        for step in (1, -1):
            if 0 <= cy - step <= 2:
                c = cx * 3 + cy
                corners.append(
                    send(tile(c, mx * 3 + 1), cx * 3 + cy - step, mx * 3 + 1 - step, beside_y[step])
                )

    def product(lhs, c, mx):
        cy = c % 3
        low_y, high_y = max(cy - 1, 0), min(cy + 1, 2)
        span = pl.ds((mx * 3 + low_y) * side, (high_y - low_y + 1) * side)
        return jnp.dot(lhs[:, span], right[c, span, :], preferred_element_type=jnp.float32)

    for edge in edges[:8]:
        forward(edge)
    for copy in local:
        copy.wait()
    for copy in sides:
        copy.wait_recv()
    for c in range(9):
        square[c] = product(left, c, 1)
        if c % 2 == 0 and 8 + c // 2 < len(edges):
            forward(edges[8 + c // 2])
    for copy in corners:
        copy.wait_recv()

    for c in range(9):
        total = square[c]
        for mx in (0, 2):
            if abs(mx - c // 3) <= 1:
                total = total + product(left, c, mx)
        square[c] = total
        for r in range(rows):
            down, across = pl.ds(r * width, width), pl.ds(c * side, side)
            square_b[down, across] = (
                square[c, down, :] * mask_ref[r : r + 1, across]
            ).astype(jnp.bfloat16)
    for c in range(9):
        total = product(square_b, c, 1)
        for mx in (0, 2):
            if abs(mx - c // 3) <= 1:
                total = total + product(square_b, c, mx)
        total = 3.0 * square[c] - 2.0 * total
        for r in range(rows):
            for q in range(rows):
                out_ref[(c * rows + q) * rows + r] = total[
                    r * width : (r + 1) * width, q * width : (q + 1) * width
                ]
    for copy in sends:
        copy.wait_send()


def pick_kernel(index_ref, dense_ref, out_ref, sem):
    count = out_ref.shape[0]

    def start(i, carry):
        pltpu.make_async_copy(dense_ref.at[index_ref[i]], out_ref.at[i], sem.at[i]).start()
        return carry

    def wait(i, carry):
        pltpu.make_async_copy(dense_ref.at[index_ref[i]], out_ref.at[i], sem.at[i]).wait()
        return carry

    lax.fori_loop(0, count, start, 0)
    lax.fori_loop(0, count, wait, 0)


def in_vmem():
    return pl.BlockSpec(memory_space=pltpu.VMEM)


def in_smem():
    return pl.BlockSpec(memory_space=pltpu.SMEM)


def per_device(density, neighbours, ent_blocks, ent_owner, ent_place):
    wide_count = lax.axis_size("gx")
    narrow_count = lax.axis_size("gy")
    device_count = wide_count * narrow_count
    here_x = lax.axis_index("gx")
    here_y = lax.axis_index("gy")
    self_index = here_x * narrow_count + here_y
    rows, slots, width = density.shape[2:5]
    side = rows * width
    held = ent_blocks.shape[0]

    owners = ent_owner.reshape(device_count, held)
    places = ent_place.reshape(device_count, held)
    entry_ids = jnp.arange(held, dtype=jnp.int32)
    my_owners = lax.dynamic_index_in_dim(owners, self_index, 0, False)
    earlier = entry_ids[None, :] < entry_ids[:, None]
    my_ranks = jnp.sum((my_owners[:, None] == my_owners[None, :]) & earlier, axis=1)
    send_slot = my_owners * C + my_ranks
    buffer_ids = jnp.arange(device_count * C, dtype=jnp.int32)
    send_index = jnp.sum(
        jnp.where(buffer_ids[:, None] == send_slot[None, :], entry_ids[None, :], 0), axis=1
    ).astype(jnp.int32)
    for_me = owners == self_index
    my_rank_at = jnp.sum(for_me[:, None, :] & earlier[None, :, :], axis=2)
    capacity_ids = jnp.arange(C, dtype=jnp.int32)
    picked = for_me[:, :, None] & (my_rank_at[:, :, None] == capacity_ids[None, None, :])
    slot_place = (
        jnp.sum(jnp.where(picked, places[:, :, None] + 1, 0), axis=1).reshape(-1) - 1
    ).astype(jnp.int32)

    columns = lax.dynamic_index_in_dim(
        lax.dynamic_index_in_dim(neighbours, here_x, 0, False), here_y, 0, False
    )
    near_x = (columns // (narrow_count * rows) - here_x + 1) % wide_count
    near_y = (columns // rows % narrow_count - here_y + 1) % narrow_count
    spot = (near_x * 3 + near_y) * rows + columns % rows
    slot_ids = jnp.arange(slots, dtype=jnp.int32)
    spot_ids = jnp.arange(9 * rows, dtype=jnp.int32)
    inverse = (
        jnp.sum(
            jnp.where(spot[:, :, None] == spot_ids[None, None, :], slot_ids[None, :, None] + 1, 0),
            axis=1,
        )
        - 1
    ).astype(jnp.int32)

    outgoing = pl.pallas_call(
        pack_kernel,
        out_shape=jax.ShapeDtypeStruct((device_count * C, width, width), jnp.bfloat16),
        in_specs=[in_smem(), in_vmem()],
        out_specs=in_vmem(),
        compiler_params=pltpu.CompilerParams(vmem_limit_bytes=32 * MIB),
        name="pack",
    )(send_index, ent_blocks)
    received = lax.all_to_all(outgoing, ("gx", "gy"), split_axis=0, concat_axis=0, tiled=True)
    own = pl.pallas_call(
        admit_kernel,
        out_shape=jax.ShapeDtypeStruct((9, side, side), jnp.bfloat16),
        in_specs=[in_smem(), in_smem(), in_vmem(), in_vmem()],
        out_specs=in_vmem(),
        scratch_shapes=[pltpu.VMEM((rows * slots, width, width), jnp.float32)],
        compiler_params=pltpu.CompilerParams(vmem_limit_bytes=40 * MIB),
        name="admit",
    )(slot_place, inverse, received, density.reshape(rows * slots, width, width))

    mask = jnp.repeat((inverse >= 0).astype(jnp.float32), width, axis=1)
    dense = pl.pallas_call(
        functools.partial(exchange_kernel, rows, wide_count, narrow_count),
        out_shape=jax.ShapeDtypeStruct((9 * rows * rows, width, width), jnp.float32),
        in_specs=[pl.BlockSpec(memory_space=pl.ANY), in_vmem()],
        out_specs=in_vmem(),
        scratch_shapes=[
            pltpu.VMEM((side, 9 * side), jnp.bfloat16),
            pltpu.VMEM((9, 9 * side, side), jnp.bfloat16),
            pltpu.VMEM((9, side, side), jnp.float32),
            pltpu.VMEM((side, 9 * side), jnp.bfloat16),
            pltpu.SemaphoreType.DMA((18,)),
            pltpu.SemaphoreType.DMA((40,)),
            pltpu.SemaphoreType.DMA((40,)),
        ],
        compiler_params=pltpu.CompilerParams(
            vmem_limit_bytes=56 * MIB, collective_id=0, has_side_effects=True
        ),
        name="exchange",
    )(own, mask)
    row_ids = jnp.arange(rows, dtype=jnp.int32)
    index = (spot * rows + row_ids[:, None]).reshape(-1).astype(jnp.int32)
    purified = pl.pallas_call(
        pick_kernel,
        out_shape=jax.ShapeDtypeStruct((rows * slots, width, width), jnp.float32),
        in_specs=[in_smem(), pl.BlockSpec(memory_space=pl.ANY)],
        out_specs=pl.BlockSpec(memory_space=pl.ANY),
        scratch_shapes=[pltpu.SemaphoreType.DMA((rows * slots,))],
        name="pick",
    )(index, dense)
    return purified.reshape(density.shape)


def solution(mesh):
    in_specs = (P("gx", "gy", None, None, None, None), P(), P(("gx", "gy"), None, None), P(), P())
    out_specs = P("gx", "gy", None, None, None, None)
    return jax.shard_map(
        per_device, mesh=mesh, in_specs=in_specs, out_specs=out_specs, check_vma=False
    )
```

```python
import functools

import jax
import jax.numpy as jnp
from jax import lax
from jax.experimental import pallas as pl
from jax.experimental.pallas import tpu as pltpu
from jax.sharding import PartitionSpec as P

C = 2
MIB = 1024 * 1024


def pack_kernel(index_ref, ent_ref, out_ref):
    def body(i, carry):
        out_ref[i] = ent_ref[index_ref[i]]
        return carry

    lax.fori_loop(0, out_ref.shape[0], body, 0)


def admit_kernel(place_ref, inverse_ref, received_ref, density_ref, own_ref, total):
    rows, slots = inverse_ref.shape[0], density_ref.shape[0] // inverse_ref.shape[0]
    width = density_ref.shape[1]

    def widen(i, carry):
        total[i] = density_ref[i].astype(jnp.float32)
        return carry

    lax.fori_loop(0, density_ref.shape[0], widen, 0)

    def add(j, carry):
        place = place_ref[j]

        @pl.when(place >= 0)
        def _():
            total[place] += received_ref[j].astype(jnp.float32)

        return carry

    lax.fori_loop(0, received_ref.shape[0], add, 0)

    def spread(near, carry):
        for r in range(rows):
            for c in range(rows):
                slot = inverse_ref[r, near * rows + c]
                spot = (near, pl.ds(r * width, width), pl.ds(c * width, width))

                @pl.when(slot >= 0)
                def _():
                    own_ref[spot] = total[r * slots + slot].astype(jnp.bfloat16)

                @pl.when(slot < 0)
                def _():
                    own_ref[spot] = jnp.zeros((width, width), jnp.bfloat16)

        return carry

    lax.fori_loop(0, 9, spread, 0)


def exchange_kernel(
    rows, gx_count, gy_count, own_ref, mask_ref, out_ref,
    left, right, square, square_b, local_sem, send_sem, recv_sem,
):
    side = left.shape[0]
    width = side // rows
    here_x, here_y = lax.axis_index("gx"), lax.axis_index("gy")
    beside_x = {
        1: (lax.rem(here_x + 1, gx_count), here_y),
        -1: (lax.rem(here_x + gx_count - 1, gx_count), here_y),
    }
    beside_y = {
        1: (here_x, lax.rem(here_y + 1, gy_count)),
        -1: (here_x, lax.rem(here_y + gy_count - 1, gy_count)),
    }

    def tile(c, m):
        return right.at[c, pl.ds(m * side, side), :]

    local = [
        pltpu.make_async_copy(own_ref.at[m], left.at[:, pl.ds(m * side, side)], local_sem.at[m])
        for m in range(9)
    ] + [
        pltpu.make_async_copy(own_ref.at[c], tile(c, 4), local_sem.at[9 + c]) for c in range(9)
    ]

    sends = []

    def send(source, c, m, device):
        copy = pltpu.make_async_remote_copy(
            src_ref=source,
            dst_ref=tile(c, m),
            send_sem=send_sem.at[len(sends)],
            recv_sem=recv_sem.at[len(sends)],
            device_id=device,
            device_id_type=pl.DeviceIdType.MESH,
        )
        sends.append(copy)
        copy.start()
        return copy

    barrier = pltpu.get_barrier_semaphore()
    for device in (*beside_x.values(), *beside_y.values()):
        pl.semaphore_signal(barrier, inc=1, device_id=device, device_id_type=pl.DeviceIdType.MESH)
    pl.semaphore_wait(barrier, 4)

    pairs = [(qy, part) for qy in (1, 0, 2) for part in (0, 1)]
    edges = []

    def send_pair(j):
        qy, part = pairs[j]
        pair = []
        for step in (1, -1):
            qx = part + 1 if step == 1 else part
            cx, mx = qx - step, 1 - step
            copy = send(own_ref.at[qx * 3 + qy], cx * 3 + qy, mx * 3 + 1, beside_x[step])
            pair.append((copy, cx, qy, mx))
        edges.append(pair)

    send_pair(0)
    send_pair(1)
    sides = []
    for qx in (1, 0, 2):
        for part in (0, 1):
            for step in (1, -1):
                qy = part + 1 if step == 1 else part
                c = qx * 3 + qy - step
                sides.append(send(own_ref.at[qx * 3 + qy], c, 4 - step, beside_y[step]))
    for copy in local:
        copy.start()

    corners = []

    def forward(edge):
        copy, cx, cy, mx = edge
        copy.wait_recv()
        for step in (1, -1):
            if 0 <= cy - step <= 2:
                c = cx * 3 + cy
                corners.append(
                    send(tile(c, mx * 3 + 1), cx * 3 + cy - step, mx * 3 + 1 - step, beside_y[step])
                )

    def product(lhs, c, mx):
        cy = c % 3
        low_y, high_y = max(cy - 1, 0), min(cy + 1, 2)
        span = pl.ds((mx * 3 + low_y) * side, (high_y - low_y + 1) * side)
        return jnp.dot(lhs[:, span], right[c, span, :], preferred_element_type=jnp.float32)

    def turn(j):
        for edge in edges[j]:
            edge[0].wait_send()
        if j + 2 < len(pairs):
            send_pair(j + 2)
        for edge in edges[j]:
            forward(edge)

    for j in range(4):
        turn(j)
    for copy in local:
        copy.wait()
    for copy in sides:
        copy.wait_recv()
    for c in range(9):
        square[c] = product(left, c, 1)
        if c in (1, 5):
            turn(4 + c // 4)
    for copy in corners:
        copy.wait_recv()

    for c in range(9):
        total = square[c]
        for mx in (0, 2):
            if abs(mx - c // 3) <= 1:
                total = total + product(left, c, mx)
        square[c] = total
        for r in range(rows):
            down, across = pl.ds(r * width, width), pl.ds(c * side, side)
            square_b[down, across] = (
                square[c, down, :] * mask_ref[r : r + 1, across]
            ).astype(jnp.bfloat16)
    for c in range(9):
        total = product(square_b, c, 1)
        for mx in (0, 2):
            if abs(mx - c // 3) <= 1:
                total = total + product(square_b, c, mx)
        total = 3.0 * square[c] - 2.0 * total
        for r in range(rows):
            for q in range(rows):
                out_ref[(c * rows + q) * rows + r] = total[
                    r * width : (r + 1) * width, q * width : (q + 1) * width
                ]
    for copy in sides + corners:
        copy.wait_send()


def pick_kernel(index_ref, dense_ref, out_ref):
    def body(i, carry):
        out_ref[i] = dense_ref[index_ref[i]]
        return carry

    lax.fori_loop(0, out_ref.shape[0], body, 0)


def in_vmem():
    return pl.BlockSpec(memory_space=pltpu.VMEM)


def in_smem():
    return pl.BlockSpec(memory_space=pltpu.SMEM)


def per_device(density, neighbours, ent_blocks, ent_owner, ent_place):
    wide_count = lax.axis_size("gx")
    narrow_count = lax.axis_size("gy")
    device_count = wide_count * narrow_count
    here_x = lax.axis_index("gx")
    here_y = lax.axis_index("gy")
    self_index = here_x * narrow_count + here_y
    rows, slots, width = density.shape[2:5]
    side = rows * width
    held = ent_blocks.shape[0]

    owners = ent_owner.reshape(device_count, held)
    places = ent_place.reshape(device_count, held)
    entry_ids = jnp.arange(held, dtype=jnp.int32)
    my_owners = lax.dynamic_index_in_dim(owners, self_index, 0, False)
    earlier = entry_ids[None, :] < entry_ids[:, None]
    my_ranks = jnp.sum((my_owners[:, None] == my_owners[None, :]) & earlier, axis=1)
    send_slot = my_owners * C + my_ranks
    buffer_ids = jnp.arange(device_count * C, dtype=jnp.int32)
    send_index = jnp.sum(
        jnp.where(buffer_ids[:, None] == send_slot[None, :], entry_ids[None, :], 0), axis=1
    ).astype(jnp.int32)
    for_me = owners == self_index
    my_rank_at = jnp.sum(for_me[:, None, :] & earlier[None, :, :], axis=2)
    capacity_ids = jnp.arange(C, dtype=jnp.int32)
    picked = for_me[:, :, None] & (my_rank_at[:, :, None] == capacity_ids[None, None, :])
    slot_place = (
        jnp.sum(jnp.where(picked, places[:, :, None] + 1, 0), axis=1).reshape(-1) - 1
    ).astype(jnp.int32)

    columns = lax.dynamic_index_in_dim(
        lax.dynamic_index_in_dim(neighbours, here_x, 0, False), here_y, 0, False
    )
    near_x = (columns // (narrow_count * rows) - here_x + 1) % wide_count
    near_y = (columns // rows % narrow_count - here_y + 1) % narrow_count
    spot = (near_x * 3 + near_y) * rows + columns % rows
    slot_ids = jnp.arange(slots, dtype=jnp.int32)
    spot_ids = jnp.arange(9 * rows, dtype=jnp.int32)
    inverse = (
        jnp.sum(
            jnp.where(spot[:, :, None] == spot_ids[None, None, :], slot_ids[None, :, None] + 1, 0),
            axis=1,
        )
        - 1
    ).astype(jnp.int32)

    outgoing = pl.pallas_call(
        pack_kernel,
        out_shape=jax.ShapeDtypeStruct((device_count * C, width, width), jnp.bfloat16),
        in_specs=[in_smem(), in_vmem()],
        out_specs=in_vmem(),
        compiler_params=pltpu.CompilerParams(vmem_limit_bytes=32 * MIB),
        name="pack",
    )(send_index, ent_blocks)
    received = lax.all_to_all(outgoing, ("gx", "gy"), split_axis=0, concat_axis=0, tiled=True)
    own = pl.pallas_call(
        admit_kernel,
        out_shape=jax.ShapeDtypeStruct((9, side, side), jnp.bfloat16),
        in_specs=[in_smem(), in_smem(), in_vmem(), in_vmem()],
        out_specs=in_vmem(),
        scratch_shapes=[pltpu.VMEM((rows * slots, width, width), jnp.float32)],
        compiler_params=pltpu.CompilerParams(vmem_limit_bytes=40 * MIB),
        name="admit",
    )(slot_place, inverse, received, density.reshape(rows * slots, width, width))

    mask = jnp.repeat((inverse >= 0).astype(jnp.float32), width, axis=1)
    dense = pl.pallas_call(
        functools.partial(exchange_kernel, rows, wide_count, narrow_count),
        out_shape=jax.ShapeDtypeStruct((9 * rows * rows, width, width), jnp.float32),
        in_specs=[pl.BlockSpec(memory_space=pl.ANY), in_vmem()],
        out_specs=in_vmem(),
        scratch_shapes=[
            pltpu.VMEM((side, 9 * side), jnp.bfloat16),
            pltpu.VMEM((9, 9 * side, side), jnp.bfloat16),
            pltpu.VMEM((9, side, side), jnp.float32),
            pltpu.VMEM((side, 9 * side), jnp.bfloat16),
            pltpu.SemaphoreType.DMA((18,)),
            pltpu.SemaphoreType.DMA((40,)),
            pltpu.SemaphoreType.DMA((40,)),
        ],
        compiler_params=pltpu.CompilerParams(
            vmem_limit_bytes=56 * MIB, collective_id=0, has_side_effects=True
        ),
        name="exchange",
    )(own, mask)
    row_ids = jnp.arange(rows, dtype=jnp.int32)
    index = (spot * rows + row_ids[:, None]).reshape(-1).astype(jnp.int32)
    purified = pl.pallas_call(
        pick_kernel,
        out_shape=jax.ShapeDtypeStruct((rows * slots, width, width), jnp.float32),
        in_specs=[in_smem(), in_vmem()],
        out_specs=in_vmem(),
        compiler_params=pltpu.CompilerParams(vmem_limit_bytes=32 * MIB),
        name="pick",
    )(index, dense)
    return purified.reshape(density.shape)


def solution(mesh):
    in_specs = (P("gx", "gy", None, None, None, None), P(), P(("gx", "gy"), None, None), P(), P())
    out_specs = P("gx", "gy", None, None, None, None)
    return jax.shard_map(
        per_device, mesh=mesh, in_specs=in_specs, out_specs=out_specs, check_vma=False
    )
```

```python
import functools

import jax
import jax.numpy as jnp
from jax import lax
from jax.experimental import pallas as pl
from jax.experimental.pallas import tpu as pltpu
from jax.sharding import PartitionSpec as P

C = 2
MIB = 1024 * 1024


def pack_kernel(index_ref, ent_ref, out_ref):
    def body(i, carry):
        out_ref[i] = ent_ref[index_ref[i]]
        return carry

    lax.fori_loop(0, out_ref.shape[0], body, 0)


def admit_kernel(place_ref, inverse_ref, received_ref, density_ref, own_ref, total):
    rows, slots = inverse_ref.shape[0], density_ref.shape[0] // inverse_ref.shape[0]
    width = density_ref.shape[1]

    def widen(i, carry):
        total[i] = density_ref[i].astype(jnp.float32)
        return carry

    lax.fori_loop(0, density_ref.shape[0], widen, 0)

    def add(j, carry):
        place = place_ref[j]

        @pl.when(place >= 0)
        def _():
            total[place] += received_ref[j].astype(jnp.float32)

        return carry

    lax.fori_loop(0, received_ref.shape[0], add, 0)

    def spread(near, carry):
        for r in range(rows):
            for c in range(rows):
                slot = inverse_ref[r, near * rows + c]
                spot = (near, pl.ds(r * width, width), pl.ds(c * width, width))

                @pl.when(slot >= 0)
                def _():
                    own_ref[spot] = total[r * slots + slot].astype(jnp.bfloat16)

                @pl.when(slot < 0)
                def _():
                    own_ref[spot] = jnp.zeros((width, width), jnp.bfloat16)

        return carry

    lax.fori_loop(0, 9, spread, 0)


def exchange_kernel(
    rows, gx_count, gy_count, own_ref, mask_ref, out_ref,
    left, right, square, square_b, local_sem, send_sem, recv_sem,
):
    side = left.shape[0]
    width = side // rows
    here_x, here_y = lax.axis_index("gx"), lax.axis_index("gy")
    beside_x = {
        1: (lax.rem(here_x + 1, gx_count), here_y),
        -1: (lax.rem(here_x + gx_count - 1, gx_count), here_y),
    }
    beside_y = {
        1: (here_x, lax.rem(here_y + 1, gy_count)),
        -1: (here_x, lax.rem(here_y + gy_count - 1, gy_count)),
    }

    def tile(c, m):
        return right.at[c, pl.ds(m * side, side), :]

    local = [
        pltpu.make_async_copy(own_ref.at[m], left.at[:, pl.ds(m * side, side)], local_sem.at[m])
        for m in range(9)
    ] + [
        pltpu.make_async_copy(own_ref.at[c], tile(c, 4), local_sem.at[9 + c]) for c in range(9)
    ]

    sends = []

    def send(source, c, m, device):
        copy = pltpu.make_async_remote_copy(
            src_ref=source,
            dst_ref=tile(c, m),
            send_sem=send_sem.at[len(sends)],
            recv_sem=recv_sem.at[len(sends)],
            device_id=device,
            device_id_type=pl.DeviceIdType.MESH,
        )
        sends.append(copy)
        copy.start()
        return copy

    barrier = pltpu.get_barrier_semaphore()
    for device in (*beside_x.values(), *beside_y.values()):
        pl.semaphore_signal(barrier, inc=1, device_id=device, device_id_type=pl.DeviceIdType.MESH)
    pl.semaphore_wait(barrier, 4)

    pairs = [(qy, part) for qy in (1, 0, 2) for part in (0, 1)]
    edges = []

    def send_pair(j):
        qy, part = pairs[j]
        pair = []
        for step in (1, -1):
            qx = part + 1 if step == 1 else part
            cx, mx = qx - step, 1 - step
            copy = send(own_ref.at[qx * 3 + qy], cx * 3 + qy, mx * 3 + 1, beside_x[step])
            pair.append((copy, cx, qy, mx))
        edges.append(pair)

    send_pair(0)
    send_pair(1)
    sides = []
    for qx in (1, 0, 2):
        for part in (0, 1):
            for step in (1, -1):
                qy = part + 1 if step == 1 else part
                c = qx * 3 + qy - step
                sides.append(send(own_ref.at[qx * 3 + qy], c, 4 - step, beside_y[step]))
    for copy in local:
        copy.start()

    corners = []

    def forward(edge):
        copy, cx, cy, mx = edge
        copy.wait_recv()
        for step in (1, -1):
            if 0 <= cy - step <= 2:
                c = cx * 3 + cy
                corners.append(
                    send(tile(c, mx * 3 + 1), cx * 3 + cy - step, mx * 3 + 1 - step, beside_y[step])
                )

    def product(lhs, c, mx):
        cy = c % 3
        low_y, high_y = max(cy - 1, 0), min(cy + 1, 2)
        span = pl.ds((mx * 3 + low_y) * side, (high_y - low_y + 1) * side)
        return jnp.dot(lhs[:, span], right[c, span, :], preferred_element_type=jnp.float32)

    def turn(j):
        for edge in edges[j]:
            edge[0].wait_send()
        if j + 2 < len(pairs):
            send_pair(j + 2)
        for edge in edges[j]:
            forward(edge)

    for j in range(len(pairs)):
        turn(j)
    for copy in local:
        copy.wait()
    for copy in sides:
        copy.wait_recv()
    for c in range(9):
        square[c] = product(left, c, 1)
    for copy in corners:
        copy.wait_recv()

    for c in range(9):
        total = square[c]
        for mx in (0, 2):
            if abs(mx - c // 3) <= 1:
                total = total + product(left, c, mx)
        square[c] = total
        for r in range(rows):
            down, across = pl.ds(r * width, width), pl.ds(c * side, side)
            square_b[down, across] = (
                square[c, down, :] * mask_ref[r : r + 1, across]
            ).astype(jnp.bfloat16)
    for c in range(9):
        total = product(square_b, c, 1)
        for mx in (0, 2):
            if abs(mx - c // 3) <= 1:
                total = total + product(square_b, c, mx)
        total = 3.0 * square[c] - 2.0 * total
        for r in range(rows):
            for q in range(rows):
                out_ref[(r * 9 + c) * rows + q] = total[
                    r * width : (r + 1) * width, q * width : (q + 1) * width
                ]
    for copy in sides + corners:
        copy.wait_send()


def pick_kernel(index_ref, dense_ref, out_ref):
    row = pl.program_id(0)

    def body(i, carry):
        out_ref[i] = dense_ref[index_ref[row, i]]
        return carry

    lax.fori_loop(0, out_ref.shape[0], body, 0)


def in_vmem():
    return pl.BlockSpec(memory_space=pltpu.VMEM)


def in_smem():
    return pl.BlockSpec(memory_space=pltpu.SMEM)


def per_device(density, neighbours, ent_blocks, ent_owner, ent_place):
    wide_count = lax.axis_size("gx")
    narrow_count = lax.axis_size("gy")
    device_count = wide_count * narrow_count
    here_x = lax.axis_index("gx")
    here_y = lax.axis_index("gy")
    self_index = here_x * narrow_count + here_y
    rows, slots, width = density.shape[2:5]
    side = rows * width
    held = ent_blocks.shape[0]

    owners = ent_owner.reshape(device_count, held)
    places = ent_place.reshape(device_count, held)
    entry_ids = jnp.arange(held, dtype=jnp.int32)
    my_owners = lax.dynamic_index_in_dim(owners, self_index, 0, False)
    earlier = entry_ids[None, :] < entry_ids[:, None]
    my_ranks = jnp.sum((my_owners[:, None] == my_owners[None, :]) & earlier, axis=1)
    send_slot = my_owners * C + my_ranks
    buffer_ids = jnp.arange(device_count * C, dtype=jnp.int32)
    send_index = jnp.sum(
        jnp.where(buffer_ids[:, None] == send_slot[None, :], entry_ids[None, :], 0), axis=1
    ).astype(jnp.int32)
    for_me = owners == self_index
    my_rank_at = jnp.sum(for_me[:, None, :] & earlier[None, :, :], axis=2)
    capacity_ids = jnp.arange(C, dtype=jnp.int32)
    picked = for_me[:, :, None] & (my_rank_at[:, :, None] == capacity_ids[None, None, :])
    slot_place = (
        jnp.sum(jnp.where(picked, places[:, :, None] + 1, 0), axis=1).reshape(-1) - 1
    ).astype(jnp.int32)

    columns = lax.dynamic_index_in_dim(
        lax.dynamic_index_in_dim(neighbours, here_x, 0, False), here_y, 0, False
    )
    near_x = (columns // (narrow_count * rows) - here_x + 1) % wide_count
    near_y = (columns // rows % narrow_count - here_y + 1) % narrow_count
    spot = (near_x * 3 + near_y) * rows + columns % rows
    slot_ids = jnp.arange(slots, dtype=jnp.int32)
    spot_ids = jnp.arange(9 * rows, dtype=jnp.int32)
    inverse = (
        jnp.sum(
            jnp.where(spot[:, :, None] == spot_ids[None, None, :], slot_ids[None, :, None] + 1, 0),
            axis=1,
        )
        - 1
    ).astype(jnp.int32)

    outgoing = pl.pallas_call(
        pack_kernel,
        out_shape=jax.ShapeDtypeStruct((device_count * C, width, width), jnp.bfloat16),
        in_specs=[in_smem(), in_vmem()],
        out_specs=in_vmem(),
        compiler_params=pltpu.CompilerParams(vmem_limit_bytes=32 * MIB),
        name="pack",
    )(send_index, ent_blocks)
    received = lax.all_to_all(outgoing, ("gx", "gy"), split_axis=0, concat_axis=0, tiled=True)
    own = pl.pallas_call(
        admit_kernel,
        out_shape=jax.ShapeDtypeStruct((9, side, side), jnp.bfloat16),
        in_specs=[in_smem(), in_smem(), in_vmem(), in_vmem()],
        out_specs=in_vmem(),
        scratch_shapes=[pltpu.VMEM((rows * slots, width, width), jnp.float32)],
        compiler_params=pltpu.CompilerParams(vmem_limit_bytes=40 * MIB),
        name="admit",
    )(slot_place, inverse, received, density.reshape(rows * slots, width, width))

    mask = jnp.repeat((inverse >= 0).astype(jnp.float32), width, axis=1)
    dense = pl.pallas_call(
        functools.partial(exchange_kernel, rows, wide_count, narrow_count),
        out_shape=jax.ShapeDtypeStruct((9 * rows * rows, width, width), jnp.float32),
        in_specs=[pl.BlockSpec(memory_space=pl.ANY), in_vmem()],
        out_specs=in_vmem(),
        scratch_shapes=[
            pltpu.VMEM((side, 9 * side), jnp.bfloat16),
            pltpu.VMEM((9, 9 * side, side), jnp.bfloat16),
            pltpu.VMEM((9, side, side), jnp.float32),
            pltpu.VMEM((side, 9 * side), jnp.bfloat16),
            pltpu.SemaphoreType.DMA((18,)),
            pltpu.SemaphoreType.DMA((40,)),
            pltpu.SemaphoreType.DMA((40,)),
        ],
        compiler_params=pltpu.CompilerParams(
            vmem_limit_bytes=56 * MIB, collective_id=0, has_side_effects=True
        ),
        name="exchange",
    )(own, mask)
    purified = pl.pallas_call(
        pick_kernel,
        grid=(rows,),
        out_shape=jax.ShapeDtypeStruct((rows * slots, width, width), jnp.float32),
        in_specs=[in_smem(), pl.BlockSpec((9 * rows, width, width), lambda r: (r, 0, 0))],
        out_specs=pl.BlockSpec((slots, width, width), lambda r: (r, 0, 0)),
        compiler_params=pltpu.CompilerParams(vmem_limit_bytes=32 * MIB),
        name="pick",
    )(spot.astype(jnp.int32), dense)
    return purified.reshape(density.shape)


def solution(mesh):
    in_specs = (P("gx", "gy", None, None, None, None), P(), P(("gx", "gy"), None, None), P(), P())
    out_specs = P("gx", "gy", None, None, None, None)
    return jax.shard_map(
        per_device, mesh=mesh, in_specs=in_specs, out_specs=out_specs, check_vma=False
    )
```
